128 devices in a mesh: group: 4 (over x), local: 32 (over y, z, core).
Axes of the slice: x: 4, y: 4, z: 4, core: 2. Of those that a mesh axis runs over, the one named last changes fastest.
Arguments:
- tokens: bfloat16 [2048, 3584], P(('group', 'local')), may hold values from -6 to 6
- expert_ids: int32 [2048, 8], P(('group', 'local')), may hold values from 0 to 127, as said below
- gates: float32 [2048, 8], P(('group', 'local')), may hold values from 0.1 to 1
- w_gate: bfloat16 [128, 3584, 1024], P(('group', 'local')), may hold values from -0.09375 to 0.09375
- w_up: bfloat16 [128, 3584, 1024], P(('group', 'local')), may hold values from -0.09375 to 0.09375
- w_down: bfloat16 [128, 1024, 3584], P(('group', 'local')), may hold values from -0.1875 to 0.1875
Outputs:
- mixed: bfloat16 [2048, 3584], P(('group', 'local'))
The draws below stay inside these ranges and needn't reach their ends.
Inputs may be any that keep to these rules, and one draw needn't show every extreme that they name: `expert_ids`: each token picks 8 different experts, 4 in each of 2 different groups, expert e belonging to group floor(e / 32). Of the 16 tokens of one device at most 2 pick the same expert. One group, the same on all devices, is picked by every token, and each of its experts by exactly 2 tokens of every device.
All inputs are finite; a program needn't handle non-finite values.
Results may differ from the reference program's by a relative error of at most 0.0065.
Values may be sent and summed in bfloat16 or wider, within the bound.
No kernel may reach another device: no remote copies, remote signals or barrier semaphores. Data moves between devices by JAX's collectives and lax.ppermute only.
A program may use at most 128 MiB of HBM per device.

```python
import math
import jax
import jax.numpy as jnp
from jax import lax

D = 3584
FF = 1024
TOK_DEV = 16
TOP = 8
PER_GROUP = 4
GROUP_COUNT = 4
GROUP_EXPERTS = 32
EXPERTS = 128
CAP = 2
TOKENS = 2048
N_GROUP = 4
N_LOCAL = 32


def draw_expert_ids(key, part):
    key = jax.random.fold_in(key, 7)
    key_hot, key_other, key_perm, key_flip = jax.random.split(key, 4)
    blocks = TOKENS // TOK_DEV
    hot_group = jax.random.randint(key_hot, (), 0, N_GROUP)
    other_group = (hot_group + 1 + jax.random.randint(key_other, (blocks, TOK_DEV), 0, N_GROUP - 1)) % N_GROUP
    hot_rank = jnp.broadcast_to(jnp.arange(TOK_DEV, dtype=jnp.int32)[None, :], (blocks, TOK_DEV))
    other_hits = (other_group[:, :, None] == jnp.arange(N_GROUP, dtype=jnp.int32)[None, None, :]).astype(jnp.int32)
    other_rank = jnp.sum(jnp.cumsum(other_hits, axis=1) * other_hits, axis=2) - 1
    perm_keys = jax.random.split(key_perm, blocks * N_GROUP)
    orders = jax.vmap(lambda single: jax.random.permutation(single, N_LOCAL))(perm_keys)
    orders = orders.reshape(blocks, N_GROUP, N_LOCAL).astype(jnp.int32)
    block_index = jnp.arange(blocks, dtype=jnp.int32)[:, None]

    def choose(group_table, rank_table):
        offsets = (PER_GROUP * rank_table[:, :, None] + jnp.arange(PER_GROUP, dtype=jnp.int32)[None, None, :]) % N_LOCAL
        order_rows = orders[block_index, group_table]
        members = jnp.take_along_axis(order_rows, offsets, axis=2)
        return group_table[:, :, None] * N_LOCAL + members
    hot_table = jnp.full((blocks, TOK_DEV), hot_group, jnp.int32)
    first = choose(hot_table, hot_rank)
    second = choose(other_group.astype(jnp.int32), other_rank)
    flipped = jax.random.randint(key_flip, (blocks, TOK_DEV), 0, 2) == 1
    joined = jnp.where(flipped[:, :, None], jnp.concatenate([second, first], axis=2), jnp.concatenate([first, second], axis=2))
    return joined.reshape(TOKENS, TOP).astype(jnp.int32)


def shard_levels(own_key, extent, shards, low, top_value):
    def one(dim, blocks):
        heights = jax.random.uniform(jax.random.fold_in(jax.random.fold_in(own_key, 6), dim), (blocks,), jnp.float32, low / len(shards), top_value / len(shards))
        return jnp.repeat(jnp.exp(heights), extent[dim] // blocks).reshape((-1,) + (1,) * (len(extent) - dim - 1))

    level = one(*shards[0])
    for cut in shards[1:]:
        level = level * one(*cut)
    return level


def normal_values(own_key, shape, width, reach, cuts=(), kind=jnp.bfloat16):
    loudness = shard_levels(own_key, shape, cuts, -0.22, 0.18) if cuts else 1.0
    values = jax.random.normal(own_key, shape, jnp.float32) * width * loudness
    return jnp.minimum(jnp.maximum(values, -reach), reach).astype(kind)


def setup_inputs(seed: int = 0) -> dict:
    splits = jax.random.split(jax.random.key(seed), 7)
    return {
        "tokens": normal_values(splits[0], (TOKENS, D), 1.0, 6.0, ((0, 128),)),
        "expert_ids": draw_expert_ids(jax.random.fold_in(splits[6], 71), 0),
        "gates": jnp.clip(jnp.exp(math.log(1.0) - 2.3025851 * jax.random.uniform(splits[2], (TOKENS, TOP), jnp.float32) ** shard_levels(splits[2], (TOKENS, TOP), ((0, 128),), -0.2, 0.2)), 0.1, 1.0),
        "w_gate": normal_values(splits[3], (EXPERTS, D, FF), D ** -0.5, 0.09375, ((0, 128),)),
        "w_up": normal_values(splits[4], (EXPERTS, D, FF), D ** -0.5, 0.09375, ((0, 128),)),
        "w_down": normal_values(splits[5], (EXPERTS, FF, D), FF ** -0.5, 0.1875, ((0, 128),)),
    }


def reference(tokens, expert_ids, gates, w_gate, w_up, w_down):
    blocks = TOKENS // TOK_DEV
    picks = TOK_DEV * TOP
    flat_ids = expert_ids.reshape(blocks, picks)
    expert_range = jnp.arange(EXPERTS, dtype=jnp.int32)
    onehot = (flat_ids[:, :, None] == expert_range[None, None, :]).astype(jnp.int32)
    ranks = jnp.sum(jnp.cumsum(onehot, axis=1) * onehot, axis=2) - 1
    block_index = jnp.broadcast_to(jnp.arange(blocks, dtype=jnp.int32)[:, None], (blocks, picks))
    token_index = block_index * TOK_DEV + (jnp.arange(picks, dtype=jnp.int32) // TOP)[None, :]
    sources = jnp.full((EXPERTS, blocks, CAP), TOKENS, jnp.int32)
    sources = sources.at[flat_ids, block_index, ranks].set(token_index)
    padded = jnp.concatenate([tokens, jnp.zeros((1, D), jnp.bfloat16)], axis=0)

    def per_expert(operands):
        gate_matrix, up_matrix, down_matrix, source_rows = operands
        chosen = padded[source_rows]
        gate_part = jnp.dot(chosen, gate_matrix, preferred_element_type=jnp.float32)
        up_part = jnp.dot(chosen, up_matrix, preferred_element_type=jnp.float32)
        hidden = (jax.nn.silu(gate_part) * up_part).astype(jnp.bfloat16)
        return jnp.dot(hidden, down_matrix, preferred_element_type=jnp.float32).astype(jnp.bfloat16)

    outputs = lax.map(per_expert, (w_gate, w_up, w_down, sources.reshape(EXPERTS, blocks * CAP)))
    position = flat_ids * (blocks * CAP) + block_index * CAP + ranks
    picked = outputs.reshape(EXPERTS * blocks * CAP, D)[position.reshape(-1)]
    picked = picked.reshape(TOKENS, TOP, D).astype(jnp.float32)
    group_of = expert_ids // GROUP_EXPERTS
    total = jnp.zeros((TOKENS, D), jnp.float32)
    for group_index in range(GROUP_COUNT):
        weights = jnp.where(group_of == group_index, gates, jnp.zeros_like(gates))
        partial_sum = jnp.sum(weights[:, :, None] * picked, axis=1)
        partial_sum = lax.optimization_barrier(partial_sum.astype(jnp.bfloat16))
        total = total + partial_sum.astype(jnp.float32)
    return total.astype(jnp.bfloat16)
```

```python
import functools

import jax
import jax.numpy as jnp
from jax import lax
from jax.experimental import pallas as pl
from jax.experimental.pallas import tpu as pltpu
from jax.sharding import PartitionSpec as P

CAPACITY = 2
QUARTERS = 4
PART = CAPACITY * QUARTERS
LANES = 128
VMEM = pl.BlockSpec(memory_space=pltpu.VMEM)


def pack_kernel(ids_ref, tokens_ref, out_ref, cut):
    top, tok = ids_ref.shape
    rows = out_ref.shape[0]
    tiles = out_ref.shape[1] // LANES
    wide = QUARTERS * tok
    for q in range(QUARTERS):
        for j in range(tiles):
            column = (j * QUARTERS + q) * LANES
            cut[q * tok:(q + 1) * tok, j * LANES:(j + 1) * LANES] = tokens_ref[:, column:column + LANES]
    t_of = lax.broadcasted_iota(jnp.int32, (tok, wide), 0)
    c_of = lax.broadcasted_iota(jnp.int32, (tok, wide), 1)
    spread = (lax.rem(c_of, tok) == t_of).astype(jnp.float32)
    ids = jnp.dot(ids_ref[...].astype(jnp.float32), spread, preferred_element_type=jnp.float32).astype(jnp.int32)
    row = lax.broadcasted_iota(jnp.int32, (rows, wide), 0)
    column = lax.broadcasted_iota(jnp.int32, (rows, wide), 1)
    expert = row // PART
    picked = expert == ids[0:1, :]
    for k in range(1, top):
        picked = picked | (expert == ids[k:k + 1, :])
    a = lax.broadcasted_iota(jnp.int32, (wide, wide), 0)
    b = lax.broadcasted_iota(jnp.int32, (wide, wide), 1)
    before = ((a // tok == b // tok) & (a < b)).astype(jnp.bfloat16)
    rank = jnp.dot(picked.astype(jnp.bfloat16), before, preferred_element_type=jnp.float32)
    slot = lax.rem(row, CAPACITY)
    quarter = lax.rem(row // CAPACITY, QUARTERS)
    chosen = picked & (rank == slot.astype(jnp.float32)) & (quarter == column // tok)
    out_ref[...] = jnp.dot(
        chosen.astype(jnp.bfloat16), cut[...], preferred_element_type=jnp.float32
    ).astype(jnp.bfloat16)


def pack(ids, tokens, experts):
    tok, width = tokens.shape
    return pl.pallas_call(
        pack_kernel,
        out_shape=jax.ShapeDtypeStruct((experts * PART, width // QUARTERS), jnp.bfloat16),
        in_specs=[VMEM, VMEM],
        out_specs=VMEM,
        scratch_shapes=[pltpu.VMEM((QUARTERS * tok, width // QUARTERS), jnp.bfloat16)],
        compiler_params=pltpu.CompilerParams(vmem_limit_bytes=16 << 20),
    )(ids, tokens)


def weigh_kernel(ids_ref, gates_ref, out_ref):
    top, tok = ids_ref.shape
    rows = out_ref.shape[1]
    wide = QUARTERS * tok
    w_of = lax.broadcasted_iota(jnp.int32, (wide, tok), 0)
    t_of = lax.broadcasted_iota(jnp.int32, (wide, tok), 1)
    spread = (lax.rem(w_of, tok) == t_of).astype(jnp.float32)
    contract = (((1,), (1,)), ((), ()))
    ids = lax.dot_general(
        spread, ids_ref[...].astype(jnp.float32), contract, preferred_element_type=jnp.float32
    ).astype(jnp.int32)
    gates = lax.dot_general(
        spread, gates_ref[...], contract,
        precision=lax.Precision.HIGHEST, preferred_element_type=jnp.float32,
    )
    line = lax.broadcasted_iota(jnp.int32, (wide, rows), 0)
    row = lax.broadcasted_iota(jnp.int32, (wide, rows), 1)
    expert = row // PART
    weight = jnp.zeros((wide, rows), jnp.float32)
    picked = jnp.zeros((wide, rows), jnp.float32)
    for k in range(top):
        hit = expert == ids[:, k:k + 1]
        weight = jnp.where(hit, gates[:, k:k + 1], weight)
        picked = jnp.where(hit, 1.0, picked)
    a = lax.broadcasted_iota(jnp.int32, (wide, wide), 0)
    b = lax.broadcasted_iota(jnp.int32, (wide, wide), 1)
    before = ((a // tok == b // tok) & (b < a)).astype(jnp.bfloat16)
    rank = jnp.dot(before, picked.astype(jnp.bfloat16), preferred_element_type=jnp.float32)
    slot = lax.rem(row, CAPACITY)
    quarter = lax.rem(row // CAPACITY, QUARTERS)
    weight = jnp.where((rank == slot.astype(jnp.float32)) & (quarter == line // tok), weight, 0.0)
    high = weight.astype(jnp.bfloat16)
    out_ref[0:wide, :] = high
    out_ref[wide:2 * wide, :] = (weight - high.astype(jnp.float32)).astype(jnp.bfloat16)


def weigh(ids, gates, experts):
    tok = ids.shape[1]
    return pl.pallas_call(
        weigh_kernel,
        out_shape=jax.ShapeDtypeStruct((2 * QUARTERS * tok, experts * PART), jnp.bfloat16),
        in_specs=[VMEM, VMEM],
        out_specs=VMEM,
        compiler_params=pltpu.CompilerParams(vmem_limit_bytes=16 << 20),
    )(ids, gates)


def combine_kernel(weights_ref, returned_ref, out_ref):
    tok = out_ref.shape[0]
    wide = QUARTERS * tok
    tiles = returned_ref.shape[1] // LANES
    both = jnp.dot(weights_ref[...], returned_ref[...], preferred_element_type=jnp.float32)
    total = (both[0:wide] + both[wide:2 * wide]).astype(jnp.bfloat16)
    for q in range(QUARTERS):
        for j in range(tiles):
            column = (j * QUARTERS + q) * LANES
            out_ref[:, column:column + LANES] = total[q * tok:(q + 1) * tok, j * LANES:(j + 1) * LANES]


def combine(weights, returned, tok):
    width = returned.shape[1] * QUARTERS
    return pl.pallas_call(
        combine_kernel,
        out_shape=jax.ShapeDtypeStruct((tok, width), jnp.bfloat16),
        in_specs=[VMEM, VMEM],
        out_specs=VMEM,
        compiler_params=pltpu.CompilerParams(vmem_limit_bytes=16 << 20),
    )(weights, returned)


def expert_kernel(
    got_ref, gate_hbm, up_hbm, down_hbm, out_ref,
    gate_buf, up_buf, down_buf, wide_buf, rows_buf, hidden_buf, gate_sem, up_sem, down_sem,
):
    ff_steps, _, ff_tile = gate_buf.shape
    d_steps, _, d_tile = down_buf.shape
    rows = got_ref.shape[0]
    sources = rows // PART

    def gate_copy(f):
        return pltpu.make_async_copy(gate_hbm.at[:, pl.ds(f * ff_tile, ff_tile)], gate_buf.at[f], gate_sem.at[f])

    def up_copy(f):
        return pltpu.make_async_copy(up_hbm.at[:, pl.ds(f * ff_tile, ff_tile)], up_buf.at[f], up_sem.at[f])

    def down_copy(n):
        return pltpu.make_async_copy(down_hbm.at[:, pl.ds(n * d_tile, d_tile)], down_buf.at[n], down_sem.at[n])

    for f in range(ff_steps):
        gate_copy(f).start()
        up_copy(f).start()
    for n in range(d_steps):
        down_copy(n).start()

    for j in range(d_steps):
        wide_buf[j] = got_ref[:, j * LANES:(j + 1) * LANES].astype(jnp.float32)
    for slot in range(CAPACITY):
        for q in range(QUARTERS):
            for j in range(d_steps):
                piece = wide_buf[j, pl.ds(q * CAPACITY + slot, sources, stride=PART), :]
                column = (j * QUARTERS + q) * LANES
                rows_buf[slot * sources:(slot + 1) * sources, column:column + LANES] = piece.astype(jnp.bfloat16)

    for f in range(ff_steps):
        gate_copy(f).wait()
        gate_part = jnp.dot(rows_buf[...], gate_buf[f], preferred_element_type=jnp.float32)
        up_copy(f).wait()
        up_part = jnp.dot(rows_buf[...], up_buf[f], preferred_element_type=jnp.float32)
        hidden = gate_part / (1.0 + jnp.exp(-gate_part)) * up_part
        hidden_buf[:, f * ff_tile:(f + 1) * ff_tile] = hidden.astype(jnp.bfloat16)

    for n in range(d_steps):
        down_copy(n).wait()
        produced = jnp.dot(hidden_buf[...], down_buf[n], preferred_element_type=jnp.float32)
        for slot in range(CAPACITY):
            for q in range(QUARTERS):
                wide_buf[n, pl.ds(q * CAPACITY + slot, sources, stride=PART), :] = produced[
                    slot * sources:(slot + 1) * sources, q * LANES:(q + 1) * LANES
                ]
        out_ref[:, n * LANES:(n + 1) * LANES] = wide_buf[n].astype(jnp.bfloat16)


def expert_ffn(got, gate_matrix, up_matrix, down_matrix):
    rows, _ = got.shape
    width, ff = gate_matrix.shape
    ff_tile = 256
    d_tile = QUARTERS * LANES
    ff_steps, d_steps = ff // ff_tile, width // d_tile
    any_spec = pl.BlockSpec(memory_space=pl.ANY)
    return pl.pallas_call(
        expert_kernel,
        out_shape=jax.ShapeDtypeStruct(got.shape, jnp.bfloat16),
        in_specs=[VMEM, any_spec, any_spec, any_spec],
        out_specs=VMEM,
        scratch_shapes=[
            pltpu.VMEM((ff_steps, width, ff_tile), jnp.bfloat16),
            pltpu.VMEM((ff_steps, width, ff_tile), jnp.bfloat16),
            pltpu.VMEM((d_steps, ff, d_tile), jnp.bfloat16),
            pltpu.VMEM((d_steps, rows, LANES), jnp.float32),
            pltpu.VMEM((rows // QUARTERS, width), jnp.bfloat16),
            pltpu.VMEM((rows // QUARTERS, ff), jnp.bfloat16),
            pltpu.SemaphoreType.DMA((ff_steps,)),
            pltpu.SemaphoreType.DMA((ff_steps,)),
            pltpu.SemaphoreType.DMA((d_steps,)),
        ],
        compiler_params=pltpu.CompilerParams(vmem_limit_bytes=48 << 20),
    )(got, gate_matrix, up_matrix, down_matrix)


def swap(messages, experts):
    parts = messages.reshape(experts, PART, messages.shape[1])
    moved = lax.all_to_all(parts, ("group", "local"), split_axis=0, concat_axis=0, tiled=True)
    return moved.reshape(messages.shape)


def on_device(tokens, expert_ids, gates, w_gate, w_up, w_down):
    experts = lax.axis_size("group") * lax.axis_size("local")
    ids = expert_ids.T
    got = swap(pack(ids, tokens, experts), experts)
    produced = expert_ffn(got, w_gate[0], w_up[0], w_down[0])
    weights = weigh(ids, gates.T, experts)
    returned = swap(produced, experts)
    return combine(weights, returned, tokens.shape[0])


def solution(mesh):
    placed = (
        P(("group", "local"), None),
        P(("group", "local"), None),
        P(("group", "local"), None),
        P(("group", "local"), None, None),
        P(("group", "local"), None, None),
        P(("group", "local"), None, None),
    )
    return jax.shard_map(
        on_device,
        mesh=mesh,
        in_specs=placed,
        out_specs=P(("group", "local"), None),
        check_vma=False,
    )
```

```python
import jax
import jax.numpy as jnp
from jax import lax
from jax.experimental import pallas as pl
from jax.experimental.pallas import tpu as pltpu
from jax.sharding import PartitionSpec as P

CAPACITY = 2
QUARTERS = 4
PART = CAPACITY * QUARTERS
LANES = 128
FF_TILE = 256
AHEAD = 3
DOWN_PARTS = 3
VMEM = pl.BlockSpec(memory_space=pltpu.VMEM)
ANYWHERE = pl.BlockSpec(memory_space=pl.ANY)


def pack_kernel(ids_hbm, tokens_hbm, out_ref, ids_ref, tokens_ref, cut, sems):
    ids_copy = pltpu.make_async_copy(ids_hbm, ids_ref, sems.at[0])
    tokens_copy = pltpu.make_async_copy(tokens_hbm, tokens_ref, sems.at[1])
    ids_copy.start()
    tokens_copy.start()
    top, tok = ids_ref.shape
    rows = out_ref.shape[0]
    tiles = out_ref.shape[1] // LANES
    wide = QUARTERS * tok
    t_of = lax.broadcasted_iota(jnp.int32, (tok, wide), 0)
    c_of = lax.broadcasted_iota(jnp.int32, (tok, wide), 1)
    spread = (lax.rem(c_of, tok) == t_of).astype(jnp.float32)
    ids_copy.wait()
    ids = jnp.dot(ids_ref[...].astype(jnp.float32), spread, preferred_element_type=jnp.float32).astype(jnp.int32)
    row = lax.broadcasted_iota(jnp.int32, (rows, wide), 0)
    column = lax.broadcasted_iota(jnp.int32, (rows, wide), 1)
    expert = row // PART
    picked = expert == ids[0:1, :]
    for k in range(1, top):
        picked = picked | (expert == ids[k:k + 1, :])
    a = lax.broadcasted_iota(jnp.int32, (wide, wide), 0)
    b = lax.broadcasted_iota(jnp.int32, (wide, wide), 1)
    before = ((a // tok == b // tok) & (a < b)).astype(jnp.bfloat16)
    rank = jnp.dot(picked.astype(jnp.bfloat16), before, preferred_element_type=jnp.float32)
    slot = lax.rem(row, CAPACITY)
    quarter = lax.rem(row // CAPACITY, QUARTERS)
    chosen = picked & (rank == slot.astype(jnp.float32)) & (quarter == column // tok)
    tokens_copy.wait()
    for q in range(QUARTERS):
        for j in range(tiles):
            column = (j * QUARTERS + q) * LANES
            cut[q * tok:(q + 1) * tok, j * LANES:(j + 1) * LANES] = tokens_ref[:, column:column + LANES]
    out_ref[...] = jnp.dot(
        chosen.astype(jnp.bfloat16), cut[...], preferred_element_type=jnp.float32
    ).astype(jnp.bfloat16)


def pack(ids, tokens, experts):
    tok, width = tokens.shape
    return pl.pallas_call(
        pack_kernel,
        out_shape=jax.ShapeDtypeStruct((experts * PART, width // QUARTERS), jnp.bfloat16),
        in_specs=[ANYWHERE, ANYWHERE],
        out_specs=VMEM,
        scratch_shapes=[
            pltpu.VMEM(ids.shape, ids.dtype),
            pltpu.VMEM(tokens.shape, tokens.dtype),
            pltpu.VMEM((QUARTERS * tok, width // QUARTERS), jnp.bfloat16),
            pltpu.SemaphoreType.DMA((2,)),
        ],
        compiler_params=pltpu.CompilerParams(vmem_limit_bytes=16 << 20),
    )(ids, tokens)


def weigh(ids_ref, gates_ref, out_ref):
    top, tok = ids_ref.shape
    rows = out_ref.shape[1]
    wide = QUARTERS * tok
    w_of = lax.broadcasted_iota(jnp.int32, (wide, tok), 0)
    t_of = lax.broadcasted_iota(jnp.int32, (wide, tok), 1)
    spread = (lax.rem(w_of, tok) == t_of).astype(jnp.float32)
    contract = (((1,), (1,)), ((), ()))
    ids = lax.dot_general(
        spread, ids_ref[...].astype(jnp.float32), contract, preferred_element_type=jnp.float32
    ).astype(jnp.int32)
    gates = lax.dot_general(
        spread, gates_ref[...], contract,
        precision=lax.Precision.HIGHEST, preferred_element_type=jnp.float32,
    )
    line = lax.broadcasted_iota(jnp.int32, (wide, rows), 0)
    row = lax.broadcasted_iota(jnp.int32, (wide, rows), 1)
    expert = row // PART
    weight = jnp.zeros((wide, rows), jnp.float32)
    picked = jnp.zeros((wide, rows), jnp.float32)
    for k in range(top):
        hit = expert == ids[:, k:k + 1]
        weight = jnp.where(hit, gates[:, k:k + 1], weight)
        picked = jnp.where(hit, 1.0, picked)
    a = lax.broadcasted_iota(jnp.int32, (wide, wide), 0)
    b = lax.broadcasted_iota(jnp.int32, (wide, wide), 1)
    before = ((a // tok == b // tok) & (b < a)).astype(jnp.bfloat16)
    rank = jnp.dot(before, picked.astype(jnp.bfloat16), preferred_element_type=jnp.float32)
    slot = lax.rem(row, CAPACITY)
    quarter = lax.rem(row // CAPACITY, QUARTERS)
    weight = jnp.where((rank == slot.astype(jnp.float32)) & (quarter == line // tok), weight, 0.0)
    high = weight.astype(jnp.bfloat16)
    out_ref[0:wide, :] = high
    out_ref[wide:2 * wide, :] = (weight - high.astype(jnp.float32)).astype(jnp.bfloat16)


def combine_kernel(weights_ref, returned_ref, out_ref):
    tok = out_ref.shape[0]
    wide = QUARTERS * tok
    tiles = returned_ref.shape[1] // LANES
    both = jnp.dot(weights_ref[...], returned_ref[...], preferred_element_type=jnp.float32)
    total = (both[0:wide] + both[wide:2 * wide]).astype(jnp.bfloat16)
    for q in range(QUARTERS):
        for j in range(tiles):
            column = (j * QUARTERS + q) * LANES
            out_ref[:, column:column + LANES] = total[q * tok:(q + 1) * tok, j * LANES:(j + 1) * LANES]


def combine(weights, returned, tok):
    width = returned.shape[1] * QUARTERS
    return pl.pallas_call(
        combine_kernel,
        out_shape=jax.ShapeDtypeStruct((tok, width), jnp.bfloat16),
        in_specs=[VMEM, VMEM],
        out_specs=VMEM,
        compiler_params=pltpu.CompilerParams(vmem_limit_bytes=16 << 20),
    )(weights, returned)


def expert_kernel(
    ids_hbm, gates_hbm, got_ref, gate_hbm, up_hbm, down_hbm, out_ref, weights_ref,
    ids_ref, gates_ref, gate_buf, up_buf, down_buf, wide_buf, rows_buf, hidden_buf,
    small_sem, gate_sem, up_sem, down_sem,
):
    ff_steps, _, ff_tile = gate_buf.shape
    rows, packed = got_ref.shape
    sources = rows // PART
    tiles = packed // LANES
    d_tile = QUARTERS * LANES
    cuts = [tiles * n // DOWN_PARTS for n in range(DOWN_PARTS + 1)]

    def small_copies():
        return (
            pltpu.make_async_copy(ids_hbm, ids_ref, small_sem.at[0]),
            pltpu.make_async_copy(gates_hbm, gates_ref, small_sem.at[1]),
        )

    def in_copies(f):
        part = pl.ds(pl.multiple_of(f * ff_tile, ff_tile), ff_tile)
        return (
            pltpu.make_async_copy(gate_hbm.at[:, part], gate_buf.at[f], gate_sem.at[f]),
            pltpu.make_async_copy(up_hbm.at[:, part], up_buf.at[f], up_sem.at[f]),
        )

    def down_copy(n):
        part = pl.ds(cuts[n] * d_tile, (cuts[n + 1] - cuts[n]) * d_tile)
        return pltpu.make_async_copy(down_hbm.at[:, part], down_buf.at[:, part], down_sem.at[n])

    for copy in small_copies():
        copy.start()
    for f in range(AHEAD):
        for copy in in_copies(f):
            copy.start()

    for j in range(tiles):
        wide_buf[j] = got_ref[:, j * LANES:(j + 1) * LANES].astype(jnp.float32)
    for slot in range(CAPACITY):
        for q in range(QUARTERS):
            for j in range(tiles):
                piece = wide_buf[j, pl.ds(q * CAPACITY + slot, sources, stride=PART), :]
                column = (j * QUARTERS + q) * LANES
                rows_buf[slot * sources:(slot + 1) * sources, column:column + LANES] = piece.astype(jnp.bfloat16)
    for copy in small_copies():
        copy.wait()
    weigh(ids_ref, gates_ref, weights_ref)

    def ff_step(f, carry):
        for copy in in_copies(f):
            copy.wait()

        @pl.when(f + AHEAD < ff_steps)
        def _():
            for copy in in_copies(f + AHEAD):
                copy.start()

        @pl.when(f == 1)
        def _():
            for n in range(DOWN_PARTS):
                down_copy(n).start()

        gate_part = jnp.dot(rows_buf[...], gate_buf[f], preferred_element_type=jnp.float32)
        up_part = jnp.dot(rows_buf[...], up_buf[f], preferred_element_type=jnp.float32)
        hidden_buf[f] = (gate_part / (1.0 + jnp.exp(-gate_part)) * up_part).astype(jnp.bfloat16)
        return carry

    lax.fori_loop(0, ff_steps, ff_step, 0)
    hidden = jnp.concatenate([hidden_buf[f] for f in range(ff_steps)], axis=1)
    for n in range(DOWN_PARTS):
        down_copy(n).wait()
        for j in range(cuts[n], cuts[n + 1]):
            produced = jnp.dot(
                hidden, down_buf[:, j * d_tile:(j + 1) * d_tile], preferred_element_type=jnp.float32
            )
            for slot in range(CAPACITY):
                for q in range(QUARTERS):
                    wide_buf[j, pl.ds(q * CAPACITY + slot, sources, stride=PART), :] = produced[
                        slot * sources:(slot + 1) * sources, q * LANES:(q + 1) * LANES
                    ]
            out_ref[:, j * LANES:(j + 1) * LANES] = wide_buf[j].astype(jnp.bfloat16)


def expert_ffn(ids, gates, got, gate_matrix, up_matrix, down_matrix):
    rows, packed = got.shape
    top, tok = ids.shape
    width, ff = gate_matrix.shape
    ff_steps = ff // FF_TILE
    return pl.pallas_call(
        expert_kernel,
        out_shape=(
            jax.ShapeDtypeStruct(got.shape, jnp.bfloat16),
            jax.ShapeDtypeStruct((2 * QUARTERS * tok, rows), jnp.bfloat16),
        ),
        in_specs=[ANYWHERE, ANYWHERE, VMEM, ANYWHERE, ANYWHERE, ANYWHERE],
        out_specs=(VMEM, VMEM),
        scratch_shapes=[
            pltpu.VMEM(ids.shape, ids.dtype),
            pltpu.VMEM(gates.shape, gates.dtype),
            pltpu.VMEM((ff_steps, width, FF_TILE), jnp.bfloat16),
            pltpu.VMEM((ff_steps, width, FF_TILE), jnp.bfloat16),
            pltpu.VMEM((ff, width), jnp.bfloat16),
            pltpu.VMEM((packed // LANES, rows, LANES), jnp.float32),
            pltpu.VMEM((rows // QUARTERS, width), jnp.bfloat16),
            pltpu.VMEM((ff_steps, rows // QUARTERS, FF_TILE), jnp.bfloat16),
            pltpu.SemaphoreType.DMA((2,)),
            pltpu.SemaphoreType.DMA((ff_steps,)),
            pltpu.SemaphoreType.DMA((ff_steps,)),
            pltpu.SemaphoreType.DMA((DOWN_PARTS,)),
        ],
        compiler_params=pltpu.CompilerParams(vmem_limit_bytes=48 << 20),
    )(ids, gates, got, gate_matrix, up_matrix, down_matrix)


def swap(messages, experts):
    parts = messages.reshape(experts, PART, messages.shape[1])
    moved = lax.all_to_all(parts, ("group", "local"), split_axis=0, concat_axis=0, tiled=True)
    return moved.reshape(messages.shape)


def on_device(tokens, expert_ids, gates, w_gate, w_up, w_down):
    experts = lax.axis_size("group") * lax.axis_size("local")
    ids = expert_ids.T
    got = swap(pack(ids, tokens, experts), experts)
    produced, weights = expert_ffn(ids, gates.T, got, w_gate[0], w_up[0], w_down[0])
    returned = swap(produced, experts)
    return combine(weights, returned, tokens.shape[0])


def solution(mesh):
    placed = (
        P(("group", "local"), None),
        P(("group", "local"), None),
        P(("group", "local"), None),
        P(("group", "local"), None, None),
        P(("group", "local"), None, None),
        P(("group", "local"), None, None),
    )
    return jax.shard_map(
        on_device,
        mesh=mesh,
        in_specs=placed,
        out_specs=P(("group", "local"), None),
        check_vma=False,
    )
```

```python
import jax
import jax.numpy as jnp
from jax import lax
from jax.experimental import pallas as pl
from jax.experimental.pallas import tpu as pltpu
from jax.sharding import PartitionSpec as P

CAPACITY = 2
QUARTERS = 4
PART = CAPACITY * QUARTERS
LANES = 128
VMEM = pl.BlockSpec(memory_space=pltpu.VMEM)


def pack_kernel(ids_ref, tokens_ref, out_ref, cut):
    top, tok = ids_ref.shape
    rows = out_ref.shape[0]
    tiles = out_ref.shape[1] // LANES
    wide = QUARTERS * tok
    for q in range(QUARTERS):
        for j in range(tiles):
            column = (j * QUARTERS + q) * LANES
            cut[q * tok:(q + 1) * tok, j * LANES:(j + 1) * LANES] = tokens_ref[:, column:column + LANES]
    t_of = lax.broadcasted_iota(jnp.int32, (tok, wide), 0)
    c_of = lax.broadcasted_iota(jnp.int32, (tok, wide), 1)
    spread = (lax.rem(c_of, tok) == t_of).astype(jnp.float32)
    ids = jnp.dot(ids_ref[...].astype(jnp.float32), spread, preferred_element_type=jnp.float32).astype(jnp.int32)
    row = lax.broadcasted_iota(jnp.int32, (rows, wide), 0)
    column = lax.broadcasted_iota(jnp.int32, (rows, wide), 1)
    expert = row // PART
    picked = expert == ids[0:1, :]
    for k in range(1, top):
        picked = picked | (expert == ids[k:k + 1, :])
    a = lax.broadcasted_iota(jnp.int32, (wide, wide), 0)
    b = lax.broadcasted_iota(jnp.int32, (wide, wide), 1)
    before = ((a // tok == b // tok) & (a < b)).astype(jnp.bfloat16)
    rank = jnp.dot(picked.astype(jnp.bfloat16), before, preferred_element_type=jnp.float32)
    slot = lax.rem(row, CAPACITY)
    quarter = lax.rem(row // CAPACITY, QUARTERS)
    chosen = picked & (rank == slot.astype(jnp.float32)) & (quarter == column // tok)
    out_ref[...] = jnp.dot(
        chosen.astype(jnp.bfloat16), cut[...], preferred_element_type=jnp.float32
    ).astype(jnp.bfloat16)


def pack(ids, tokens, experts):
    tok, width = tokens.shape
    return pl.pallas_call(
        pack_kernel,
        out_shape=jax.ShapeDtypeStruct((experts * PART, width // QUARTERS), jnp.bfloat16),
        in_specs=[VMEM, VMEM],
        out_specs=VMEM,
        scratch_shapes=[pltpu.VMEM((QUARTERS * tok, width // QUARTERS), jnp.bfloat16)],
        cost_estimate=pl.CostEstimate(flops=8_000_000_000, bytes_accessed=4 << 20, transcendentals=0),
        compiler_params=pltpu.CompilerParams(vmem_limit_bytes=16 << 20),
    )(ids, tokens)


def weigh(ids_ref, gates_ref, out_ref):
    top, tok = ids_ref.shape
    rows = out_ref.shape[1]
    wide = QUARTERS * tok
    w_of = lax.broadcasted_iota(jnp.int32, (wide, tok), 0)
    t_of = lax.broadcasted_iota(jnp.int32, (wide, tok), 1)
    spread = (lax.rem(w_of, tok) == t_of).astype(jnp.float32)
    contract = (((1,), (1,)), ((), ()))
    ids = lax.dot_general(
        spread, ids_ref[...].astype(jnp.float32), contract, preferred_element_type=jnp.float32
    ).astype(jnp.int32)
    gates = lax.dot_general(
        spread, gates_ref[...], contract,
        precision=lax.Precision.HIGHEST, preferred_element_type=jnp.float32,
    )
    line = lax.broadcasted_iota(jnp.int32, (wide, rows), 0)
    row = lax.broadcasted_iota(jnp.int32, (wide, rows), 1)
    expert = row // PART
    weight = jnp.zeros((wide, rows), jnp.float32)
    picked = jnp.zeros((wide, rows), jnp.float32)
    for k in range(top):
        hit = expert == ids[:, k:k + 1]
        weight = jnp.where(hit, gates[:, k:k + 1], weight)
        picked = jnp.where(hit, 1.0, picked)
    a = lax.broadcasted_iota(jnp.int32, (wide, wide), 0)
    b = lax.broadcasted_iota(jnp.int32, (wide, wide), 1)
    before = ((a // tok == b // tok) & (b < a)).astype(jnp.bfloat16)
    rank = jnp.dot(before, picked.astype(jnp.bfloat16), preferred_element_type=jnp.float32)
    slot = lax.rem(row, CAPACITY)
    quarter = lax.rem(row // CAPACITY, QUARTERS)
    weight = jnp.where((rank == slot.astype(jnp.float32)) & (quarter == line // tok), weight, 0.0)
    high = weight.astype(jnp.bfloat16)
    out_ref[0:wide, :] = high
    out_ref[wide:2 * wide, :] = (weight - high.astype(jnp.float32)).astype(jnp.bfloat16)


def combine_kernel(weights_ref, returned_ref, out_ref):
    tok = out_ref.shape[0]
    wide = QUARTERS * tok
    tiles = returned_ref.shape[1] // LANES
    both = jnp.dot(weights_ref[...], returned_ref[...], preferred_element_type=jnp.float32)
    total = (both[0:wide] + both[wide:2 * wide]).astype(jnp.bfloat16)
    for q in range(QUARTERS):
        for j in range(tiles):
            column = (j * QUARTERS + q) * LANES
            out_ref[:, column:column + LANES] = total[q * tok:(q + 1) * tok, j * LANES:(j + 1) * LANES]


def combine(weights, returned, tok):
    width = returned.shape[1] * QUARTERS
    return pl.pallas_call(
        combine_kernel,
        out_shape=jax.ShapeDtypeStruct((tok, width), jnp.bfloat16),
        in_specs=[VMEM, VMEM],
        out_specs=VMEM,
        compiler_params=pltpu.CompilerParams(vmem_limit_bytes=16 << 20),
    )(weights, returned)


def expert_kernel(
    ids_ref, gates_ref, got_ref, gate_ref, up_ref, down_ref, out_ref, weights_ref, wide_buf, rows_buf, hidden_buf
):
    rows = got_ref.shape[0]
    sources = rows // PART
    tiles = got_ref.shape[1] // LANES
    ff_tile = 512
    d_tile = QUARTERS * LANES

    weigh(ids_ref, gates_ref, weights_ref)
    def unpack(j):
        wide_buf[j] = got_ref[:, j * LANES:(j + 1) * LANES].astype(jnp.float32)
        for slot in range(CAPACITY):
            for q in range(QUARTERS):
                piece = wide_buf[j, pl.ds(q * CAPACITY + slot, sources, stride=PART), :]
                column = (j * QUARTERS + q) * LANES
                rows_buf[slot * sources:(slot + 1) * sources, column:column + LANES] = piece.astype(jnp.bfloat16)

    def product(matrix_ref, part, low, high):
        return jnp.dot(rows_buf[:, low:high], matrix_ref[low:high, part], preferred_element_type=jnp.float32)

    for j in range(tiles):
        unpack(j)
    width = tiles * d_tile
    for f in range(gate_ref.shape[1] // ff_tile):
        part = slice(f * ff_tile, (f + 1) * ff_tile)
        gate_part = product(gate_ref, part, 0, width)
        up_part = product(up_ref, part, 0, width)
        hidden = gate_part / (1.0 + jnp.exp(-gate_part)) * up_part
        hidden_buf[:, part] = hidden.astype(jnp.bfloat16)
    for n in range(tiles):
        produced = jnp.dot(
            hidden_buf[...], down_ref[:, n * d_tile:(n + 1) * d_tile], preferred_element_type=jnp.float32
        )
        for slot in range(CAPACITY):
            for q in range(QUARTERS):
                wide_buf[n, pl.ds(q * CAPACITY + slot, sources, stride=PART), :] = produced[
                    slot * sources:(slot + 1) * sources, q * LANES:(q + 1) * LANES
                ]
        out_ref[:, n * LANES:(n + 1) * LANES] = wide_buf[n].astype(jnp.bfloat16)


def expert_ffn(ids, gates, got, gate_matrix, up_matrix, down_matrix):
    rows, packed = got.shape
    width, ff = gate_matrix.shape
    top, tok = ids.shape
    return pl.pallas_call(
        expert_kernel,
        out_shape=(
            jax.ShapeDtypeStruct(got.shape, jnp.bfloat16),
            jax.ShapeDtypeStruct((2 * QUARTERS * tok, rows), jnp.bfloat16),
        ),
        in_specs=[VMEM] * 6,
        out_specs=(VMEM, VMEM),
        scratch_shapes=[
            pltpu.VMEM((packed // LANES, rows, LANES), jnp.float32),
            pltpu.VMEM((rows // QUARTERS, width), jnp.bfloat16),
            pltpu.VMEM((rows // QUARTERS, ff), jnp.bfloat16),
        ],
        compiler_params=pltpu.CompilerParams(vmem_limit_bytes=14 << 20),
    )(ids, gates, got, gate_matrix, up_matrix, down_matrix)


def swap(messages, experts):
    parts = messages.reshape(experts, PART, messages.shape[1])
    moved = lax.all_to_all(parts, ("group", "local"), split_axis=0, concat_axis=0, tiled=True)
    return moved.reshape(messages.shape)


def on_device(tokens, expert_ids, gates, w_gate, w_up, w_down):
    experts = lax.axis_size("group") * lax.axis_size("local")
    ids = expert_ids.T
    got = swap(pack(ids, tokens, experts), experts)
    produced, weights = expert_ffn(ids, gates.T, got, w_gate[0], w_up[0], w_down[0])
    returned = swap(produced, experts)
    return combine(weights, returned, tokens.shape[0])


def solution(mesh):
    placed = (
        P(("group", "local"), None),
        P(("group", "local"), None),
        P(("group", "local"), None),
        P(("group", "local"), None, None),
        P(("group", "local"), None, None),
        P(("group", "local"), None, None),
    )
    return jax.shard_map(
        on_device,
        mesh=mesh,
        in_specs=placed,
        out_specs=P(("group", "local"), None),
        check_vma=False,
    )
```

```python
import jax
import jax.numpy as jnp
from jax import lax
from jax.experimental import pallas as pl
from jax.experimental.pallas import tpu as pltpu
from jax.sharding import PartitionSpec as P

CAPACITY = 2
QUARTERS = 4
PART = CAPACITY * QUARTERS
LANES = 128
VMEM = pl.BlockSpec(memory_space=pltpu.VMEM)


def choose_kernel(ids_ref, out_ref):
    top, tok = ids_ref.shape
    rows, wide = out_ref.shape
    t_of = lax.broadcasted_iota(jnp.int32, (tok, wide), 0)
    c_of = lax.broadcasted_iota(jnp.int32, (tok, wide), 1)
    spread = (lax.rem(c_of, tok) == t_of).astype(jnp.float32)
    ids = jnp.dot(ids_ref[...].astype(jnp.float32), spread, preferred_element_type=jnp.float32).astype(jnp.int32)
    row = lax.broadcasted_iota(jnp.int32, (rows, wide), 0)
    column = lax.broadcasted_iota(jnp.int32, (rows, wide), 1)
    expert = row // PART
    picked = expert == ids[0:1, :]
    for k in range(1, top):
        picked = picked | (expert == ids[k:k + 1, :])
    a = lax.broadcasted_iota(jnp.int32, (wide, wide), 0)
    b = lax.broadcasted_iota(jnp.int32, (wide, wide), 1)
    before = ((a // tok == b // tok) & (a < b)).astype(jnp.bfloat16)
    rank = jnp.dot(picked.astype(jnp.bfloat16), before, preferred_element_type=jnp.float32)
    slot = lax.rem(row, CAPACITY)
    quarter = lax.rem(row // CAPACITY, QUARTERS)
    chosen = picked & (rank == slot.astype(jnp.float32)) & (quarter == column // tok)
    out_ref[...] = chosen.astype(jnp.bfloat16)


def choose(ids, experts):
    tok = ids.shape[1]
    return pl.pallas_call(
        choose_kernel,
        out_shape=jax.ShapeDtypeStruct((experts * PART, QUARTERS * tok), jnp.bfloat16),
        in_specs=[VMEM],
        out_specs=VMEM,
        cost_estimate=pl.CostEstimate(flops=8_000_000_000, bytes_accessed=1 << 18, transcendentals=0),
        compiler_params=pltpu.CompilerParams(vmem_limit_bytes=8 << 20),
    )(ids)


def pack_kernel(chosen_ref, tokens_ref, out_ref, cut):
    tok = tokens_ref.shape[0]
    tiles = out_ref.shape[1] // LANES
    for q in range(QUARTERS):
        for j in range(tiles):
            column = (j * QUARTERS + q) * LANES
            cut[q * tok:(q + 1) * tok, j * LANES:(j + 1) * LANES] = tokens_ref[:, column:column + LANES]
    out_ref[...] = jnp.dot(chosen_ref[...], cut[...], preferred_element_type=jnp.float32).astype(jnp.bfloat16)


def pack(chosen, tokens):
    tok, width = tokens.shape
    return pl.pallas_call(
        pack_kernel,
        out_shape=jax.ShapeDtypeStruct((chosen.shape[0], width // QUARTERS), jnp.bfloat16),
        in_specs=[VMEM, VMEM],
        out_specs=VMEM,
        scratch_shapes=[pltpu.VMEM((QUARTERS * tok, width // QUARTERS), jnp.bfloat16)],
        cost_estimate=pl.CostEstimate(flops=8_000_000_000, bytes_accessed=4 << 20, transcendentals=0),
        compiler_params=pltpu.CompilerParams(vmem_limit_bytes=8 << 20),
    )(chosen, tokens)


def weigh(ids_ref, gates_ref, out_ref):
    top, tok = ids_ref.shape
    rows = out_ref.shape[1]
    wide = QUARTERS * tok
    w_of = lax.broadcasted_iota(jnp.int32, (wide, tok), 0)
    t_of = lax.broadcasted_iota(jnp.int32, (wide, tok), 1)
    spread = (lax.rem(w_of, tok) == t_of).astype(jnp.float32)
    contract = (((1,), (1,)), ((), ()))
    ids = lax.dot_general(
        spread, ids_ref[...].astype(jnp.float32), contract, preferred_element_type=jnp.float32
    ).astype(jnp.int32)
    gates = lax.dot_general(
        spread, gates_ref[...], contract,
        precision=lax.Precision.HIGHEST, preferred_element_type=jnp.float32,
    )
    line = lax.broadcasted_iota(jnp.int32, (wide, rows), 0)
    row = lax.broadcasted_iota(jnp.int32, (wide, rows), 1)
    expert = row // PART
    weight = jnp.zeros((wide, rows), jnp.float32)
    picked = jnp.zeros((wide, rows), jnp.float32)
    for k in range(top):
        hit = expert == ids[:, k:k + 1]
        weight = jnp.where(hit, gates[:, k:k + 1], weight)
        picked = jnp.where(hit, 1.0, picked)
    a = lax.broadcasted_iota(jnp.int32, (wide, wide), 0)
    b = lax.broadcasted_iota(jnp.int32, (wide, wide), 1)
    before = ((a // tok == b // tok) & (b < a)).astype(jnp.bfloat16)
    rank = jnp.dot(before, picked.astype(jnp.bfloat16), preferred_element_type=jnp.float32)
    slot = lax.rem(row, CAPACITY)
    quarter = lax.rem(row // CAPACITY, QUARTERS)
    weight = jnp.where((rank == slot.astype(jnp.float32)) & (quarter == line // tok), weight, 0.0)
    high = weight.astype(jnp.bfloat16)
    out_ref[0:wide, :] = high
    out_ref[wide:2 * wide, :] = (weight - high.astype(jnp.float32)).astype(jnp.bfloat16)


def combine_kernel(weights_ref, returned_ref, out_ref):
    tok = out_ref.shape[0]
    wide = QUARTERS * tok
    tiles = returned_ref.shape[1] // LANES
    both = jnp.dot(weights_ref[...], returned_ref[...], preferred_element_type=jnp.float32)
    total = (both[0:wide] + both[wide:2 * wide]).astype(jnp.bfloat16)
    for q in range(QUARTERS):
        for j in range(tiles):
            column = (j * QUARTERS + q) * LANES
            out_ref[:, column:column + LANES] = total[q * tok:(q + 1) * tok, j * LANES:(j + 1) * LANES]


def combine(weights, returned, tok):
    width = returned.shape[1] * QUARTERS
    return pl.pallas_call(
        combine_kernel,
        out_shape=jax.ShapeDtypeStruct((tok, width), jnp.bfloat16),
        in_specs=[VMEM, VMEM],
        out_specs=VMEM,
        compiler_params=pltpu.CompilerParams(vmem_limit_bytes=16 << 20),
    )(weights, returned)


def expert_kernel(
    ids_ref, gates_ref, got_ref, gate_ref, up_ref, down_ref, out_ref, weights_ref, wide_buf, rows_buf, hidden_buf
):
    rows = got_ref.shape[0]
    sources = rows // PART
    tiles = got_ref.shape[1] // LANES
    ff_tile = 512
    d_tile = QUARTERS * LANES

    weigh(ids_ref, gates_ref, weights_ref)
    def unpack(j):
        wide_buf[j] = got_ref[:, j * LANES:(j + 1) * LANES].astype(jnp.float32)
        for slot in range(CAPACITY):
            for q in range(QUARTERS):
                piece = wide_buf[j, pl.ds(q * CAPACITY + slot, sources, stride=PART), :]
                column = (j * QUARTERS + q) * LANES
                rows_buf[slot * sources:(slot + 1) * sources, column:column + LANES] = piece.astype(jnp.bfloat16)

    def product(matrix_ref, part, low, high):
        return jnp.dot(rows_buf[:, low:high], matrix_ref[low:high, part], preferred_element_type=jnp.float32)

    for j in range(tiles):
        unpack(j)
    width = tiles * d_tile
    for f in range(gate_ref.shape[1] // ff_tile):
        part = slice(f * ff_tile, (f + 1) * ff_tile)
        gate_part = product(gate_ref, part, 0, width)
        up_part = product(up_ref, part, 0, width)
        hidden = gate_part / (1.0 + jnp.exp(-gate_part)) * up_part
        hidden_buf[:, part] = hidden.astype(jnp.bfloat16)
    for n in range(tiles):
        produced = jnp.dot(
            hidden_buf[...], down_ref[:, n * d_tile:(n + 1) * d_tile], preferred_element_type=jnp.float32
        )
        for slot in range(CAPACITY):
            for q in range(QUARTERS):
                wide_buf[n, pl.ds(q * CAPACITY + slot, sources, stride=PART), :] = produced[
                    slot * sources:(slot + 1) * sources, q * LANES:(q + 1) * LANES
                ]
        out_ref[:, n * LANES:(n + 1) * LANES] = wide_buf[n].astype(jnp.bfloat16)


def expert_ffn(ids, gates, got, gate_matrix, up_matrix, down_matrix):
    rows, packed = got.shape
    width, ff = gate_matrix.shape
    top, tok = ids.shape
    return pl.pallas_call(
        expert_kernel,
        out_shape=(
            jax.ShapeDtypeStruct(got.shape, jnp.bfloat16),
            jax.ShapeDtypeStruct((2 * QUARTERS * tok, rows), jnp.bfloat16),
        ),
        in_specs=[VMEM] * 6,
        out_specs=(VMEM, VMEM),
        scratch_shapes=[
            pltpu.VMEM((packed // LANES, rows, LANES), jnp.float32),
            pltpu.VMEM((rows // QUARTERS, width), jnp.bfloat16),
            pltpu.VMEM((rows // QUARTERS, ff), jnp.bfloat16),
        ],
        compiler_params=pltpu.CompilerParams(vmem_limit_bytes=14 << 20),
    )(ids, gates, got, gate_matrix, up_matrix, down_matrix)


def swap(messages, experts):
    parts = messages.reshape(experts, PART, messages.shape[1])
    moved = lax.all_to_all(parts, ("group", "local"), split_axis=0, concat_axis=0, tiled=True)
    return moved.reshape(messages.shape)


def on_device(tokens, expert_ids, gates, w_gate, w_up, w_down):
    experts = lax.axis_size("group") * lax.axis_size("local")
    ids = expert_ids.T
    got = swap(pack(choose(ids, experts), tokens), experts)
    produced, weights = expert_ffn(ids, gates.T, got, w_gate[0], w_up[0], w_down[0])
    returned = swap(produced, experts)
    return combine(weights, returned, tokens.shape[0])


def solution(mesh):
    placed = (
        P(("group", "local"), None),
        P(("group", "local"), None),
        P(("group", "local"), None),
        P(("group", "local"), None, None),
        P(("group", "local"), None, None),
        P(("group", "local"), None, None),
    )
    return jax.shard_map(
        on_device,
        mesh=mesh,
        in_specs=placed,
        out_specs=P(("group", "local"), None),
        check_vma=False,
    )
```

```python
import jax
import jax.numpy as jnp
from jax import lax
from jax.experimental import pallas as pl
from jax.experimental.pallas import tpu as pltpu
from jax.sharding import PartitionSpec as P

CAPACITY = 2
QUARTERS = 4
PART = CAPACITY * QUARTERS
LANES = 128
VMEM = pl.BlockSpec(memory_space=pltpu.VMEM)


def turned(values):
    tok = values.shape[1]
    a = lax.broadcasted_iota(jnp.int32, (tok, tok), 0)
    b = lax.broadcasted_iota(jnp.int32, (tok, tok), 1)
    return lax.dot_general(
        (a == b).astype(jnp.float32), values, (((1,), (1,)), ((), ())),
        precision=lax.Precision.HIGHEST, preferred_element_type=jnp.float32,
    )


def choose_kernel(ids_ref, out_ref):
    top, tok = ids_ref.shape
    rows = out_ref.shape[1]
    ids = turned(ids_ref[...]).astype(jnp.int32)
    row = lax.broadcasted_iota(jnp.int32, (tok, rows), 1)
    expert = row // PART
    picked = expert == ids[:, 0:1]
    for k in range(1, top):
        picked = picked | (expert == ids[:, k:k + 1])
    a = lax.broadcasted_iota(jnp.int32, (tok, tok), 0)
    b = lax.broadcasted_iota(jnp.int32, (tok, tok), 1)
    before = (b < a).astype(jnp.bfloat16)
    rank = jnp.dot(before, picked.astype(jnp.bfloat16), preferred_element_type=jnp.float32)
    slot = lax.rem(row, CAPACITY)
    quarter = lax.rem(row // CAPACITY, QUARTERS)
    chosen = picked & (rank == slot.astype(jnp.float32))
    for q in range(QUARTERS):
        out_ref[q * tok:(q + 1) * tok, :] = (chosen & (quarter == q)).astype(jnp.bfloat16)


def choose(ids, experts):
    tok = ids.shape[1]
    return pl.pallas_call(
        choose_kernel,
        out_shape=jax.ShapeDtypeStruct((QUARTERS * tok, experts * PART), jnp.bfloat16),
        in_specs=[VMEM],
        out_specs=VMEM,
        cost_estimate=pl.CostEstimate(flops=8_000_000_000, bytes_accessed=1 << 18, transcendentals=0),
        compiler_params=pltpu.CompilerParams(vmem_limit_bytes=8 << 20),
    )(ids)


def pack_kernel(chosen_ref, tokens_ref, out_ref, cut):
    tok = tokens_ref.shape[0]
    tiles = out_ref.shape[1] // LANES
    for q in range(QUARTERS):
        for j in range(tiles):
            column = (j * QUARTERS + q) * LANES
            cut[q * tok:(q + 1) * tok, j * LANES:(j + 1) * LANES] = tokens_ref[:, column:column + LANES]
    out_ref[...] = lax.dot_general(
        chosen_ref[...], cut[...], (((0,), (0,)), ((), ())), preferred_element_type=jnp.float32
    ).astype(jnp.bfloat16)


def pack(chosen, tokens):
    tok, width = tokens.shape
    return pl.pallas_call(
        pack_kernel,
        out_shape=jax.ShapeDtypeStruct((chosen.shape[1], width // QUARTERS), jnp.bfloat16),
        in_specs=[VMEM, VMEM],
        out_specs=VMEM,
        scratch_shapes=[pltpu.VMEM((QUARTERS * tok, width // QUARTERS), jnp.bfloat16)],
        cost_estimate=pl.CostEstimate(flops=8_000_000_000, bytes_accessed=4 << 20, transcendentals=0),
        compiler_params=pltpu.CompilerParams(vmem_limit_bytes=8 << 20),
    )(chosen, tokens)


def weigh(ids_ref, gates_ref, chosen_ref, out_ref):
    top, tok = ids_ref.shape
    rows = out_ref.shape[1]
    wide = QUARTERS * tok
    ids = turned(ids_ref[...]).astype(jnp.int32)
    gates = turned(gates_ref[...])
    expert = lax.broadcasted_iota(jnp.int32, (tok, rows), 1) // PART
    weight = jnp.zeros((tok, rows), jnp.float32)
    for k in range(top):
        weight = jnp.where(expert == ids[:, k:k + 1], gates[:, k:k + 1], weight)
    high = weight.astype(jnp.bfloat16)
    low = (weight - high.astype(jnp.float32)).astype(jnp.bfloat16)
    for q in range(QUARTERS):
        part = slice(q * tok, (q + 1) * tok)
        chosen = chosen_ref[part, :]
        out_ref[part, :] = high * chosen
        out_ref[wide + q * tok:wide + (q + 1) * tok, :] = low * chosen


def combine_kernel(weights_ref, returned_ref, out_ref):
    tok = out_ref.shape[0]
    wide = QUARTERS * tok
    tiles = returned_ref.shape[1] // LANES
    both = jnp.dot(weights_ref[...], returned_ref[...], preferred_element_type=jnp.float32)
    total = (both[0:wide] + both[wide:2 * wide]).astype(jnp.bfloat16)
    for q in range(QUARTERS):
        for j in range(tiles):
            column = (j * QUARTERS + q) * LANES
            out_ref[:, column:column + LANES] = total[q * tok:(q + 1) * tok, j * LANES:(j + 1) * LANES]


def combine(weights, returned, tok):
    width = returned.shape[1] * QUARTERS
    return pl.pallas_call(
        combine_kernel,
        out_shape=jax.ShapeDtypeStruct((tok, width), jnp.bfloat16),
        in_specs=[VMEM, VMEM],
        out_specs=VMEM,
        compiler_params=pltpu.CompilerParams(vmem_limit_bytes=16 << 20),
    )(weights, returned)


def expert_kernel(
    ids_ref, gates_ref, chosen_ref, got_ref, gate_ref, up_ref, down_ref, out_ref, weights_ref, wide_buf, rows_buf, hidden_buf
):
    rows = got_ref.shape[0]
    sources = rows // PART
    tiles = got_ref.shape[1] // LANES
    ff_tile = 512
    d_tile = QUARTERS * LANES

    weigh(ids_ref, gates_ref, chosen_ref, weights_ref)
    def unpack(j):
        wide_buf[j] = got_ref[:, j * LANES:(j + 1) * LANES].astype(jnp.float32)
        for slot in range(CAPACITY):
            for q in range(QUARTERS):
                piece = wide_buf[j, pl.ds(q * CAPACITY + slot, sources, stride=PART), :]
                column = (j * QUARTERS + q) * LANES
                rows_buf[slot * sources:(slot + 1) * sources, column:column + LANES] = piece.astype(jnp.bfloat16)

    def product(matrix_ref, part, low, high):
        return jnp.dot(rows_buf[:, low:high], matrix_ref[low:high, part], preferred_element_type=jnp.float32)

    for j in range(tiles):
        unpack(j)
    width = tiles * d_tile
    for f in range(gate_ref.shape[1] // ff_tile):
        part = slice(f * ff_tile, (f + 1) * ff_tile)
        gate_part = product(gate_ref, part, 0, width)
        up_part = product(up_ref, part, 0, width)
        hidden = gate_part / (1.0 + jnp.exp(-gate_part)) * up_part
        hidden_buf[:, part] = hidden.astype(jnp.bfloat16)
    for n in range(tiles):
        produced = jnp.dot(
            hidden_buf[...], down_ref[:, n * d_tile:(n + 1) * d_tile], preferred_element_type=jnp.float32
        )
        for slot in range(CAPACITY):
            for q in range(QUARTERS):
                wide_buf[n, pl.ds(q * CAPACITY + slot, sources, stride=PART), :] = produced[
                    slot * sources:(slot + 1) * sources, q * LANES:(q + 1) * LANES
                ]
        out_ref[:, n * LANES:(n + 1) * LANES] = wide_buf[n].astype(jnp.bfloat16)


def expert_ffn(ids, gates, chosen, got, gate_matrix, up_matrix, down_matrix):
    rows, packed = got.shape
    width, ff = gate_matrix.shape
    top, tok = ids.shape
    return pl.pallas_call(
        expert_kernel,
        out_shape=(
            jax.ShapeDtypeStruct(got.shape, jnp.bfloat16),
            jax.ShapeDtypeStruct((2 * QUARTERS * tok, rows), jnp.bfloat16),
        ),
        in_specs=[VMEM] * 7,
        out_specs=(VMEM, VMEM),
        scratch_shapes=[
            pltpu.VMEM((packed // LANES, rows, LANES), jnp.float32),
            pltpu.VMEM((rows // QUARTERS, width), jnp.bfloat16),
            pltpu.VMEM((rows // QUARTERS, ff), jnp.bfloat16),
        ],
        compiler_params=pltpu.CompilerParams(vmem_limit_bytes=14 << 20),
    )(ids, gates, chosen, got, gate_matrix, up_matrix, down_matrix)


def swap(messages, experts):
    parts = messages.reshape(experts, PART, messages.shape[1])
    moved = lax.all_to_all(parts, ("group", "local"), split_axis=0, concat_axis=0, tiled=True)
    return moved.reshape(messages.shape)


def on_device(tokens, expert_ids, gates, w_gate, w_up, w_down):
    experts = lax.axis_size("group") * lax.axis_size("local")
    ids = expert_ids.T.astype(jnp.float32)
    chosen = choose(ids, experts)
    got = swap(pack(chosen, tokens), experts)
    produced, weights = expert_ffn(ids, gates.T, chosen, got, w_gate[0], w_up[0], w_down[0])
    returned = swap(produced, experts)
    return combine(weights, returned, tokens.shape[0])


def solution(mesh):
    placed = (
        P(("group", "local"), None),
        P(("group", "local"), None),
        P(("group", "local"), None),
        P(("group", "local"), None, None),
        P(("group", "local"), None, None),
        P(("group", "local"), None, None),
    )
    return jax.shard_map(
        on_device,
        mesh=mesh,
        in_specs=placed,
        out_specs=P(("group", "local"), None),
        check_vma=False,
    )
```

```python
import jax
import jax.numpy as jnp
from jax import lax
from jax.experimental import pallas as pl
from jax.experimental.pallas import tpu as pltpu
from jax.sharding import PartitionSpec as P

CAPACITY = 2
QUARTERS = 4
PART = CAPACITY * QUARTERS
LANES = 128
VMEM = pl.BlockSpec(memory_space=pltpu.VMEM)


def turned(values):
    tok = values.shape[1]
    a = lax.broadcasted_iota(jnp.int32, (tok, tok), 0)
    b = lax.broadcasted_iota(jnp.int32, (tok, tok), 1)
    return lax.dot_general(
        (a == b).astype(jnp.float32), values, (((1,), (1,)), ((), ())),
        precision=lax.Precision.HIGHEST, preferred_element_type=jnp.float32,
    )


def choose_kernel(ids_ref, out_ref):
    top, tok = ids_ref.shape
    rows = out_ref.shape[1]
    ids = turned(ids_ref[...]).astype(jnp.int32)
    row = lax.broadcasted_iota(jnp.int32, (tok, rows), 1)
    expert = row // PART
    picked = expert == ids[:, 0:1]
    for k in range(1, top):
        picked = picked | (expert == ids[:, k:k + 1])
    a = lax.broadcasted_iota(jnp.int32, (tok, tok), 0)
    b = lax.broadcasted_iota(jnp.int32, (tok, tok), 1)
    before = (b < a).astype(jnp.bfloat16)
    rank = jnp.dot(before, picked.astype(jnp.bfloat16), preferred_element_type=jnp.float32)
    slot = lax.rem(row, CAPACITY)
    quarter = lax.rem(row // CAPACITY, QUARTERS)
    chosen = picked & (rank == slot.astype(jnp.float32))
    for q in range(QUARTERS):
        out_ref[q * tok:(q + 1) * tok, :] = (chosen & (quarter == q)).astype(jnp.bfloat16)


def choose(ids, experts):
    tok = ids.shape[1]
    return pl.pallas_call(
        choose_kernel,
        out_shape=jax.ShapeDtypeStruct((QUARTERS * tok, experts * PART), jnp.bfloat16),
        in_specs=[VMEM],
        out_specs=VMEM,
        cost_estimate=pl.CostEstimate(flops=8_000_000_000, bytes_accessed=1 << 18, transcendentals=0),
        compiler_params=pltpu.CompilerParams(vmem_limit_bytes=8 << 20),
    )(ids)


def pack_kernel(chosen_ref, tokens_ref, out_ref, cut):
    tok = tokens_ref.shape[0]
    tiles = out_ref.shape[1] // LANES
    for q in range(QUARTERS):
        for j in range(tiles):
            column = (j * QUARTERS + q) * LANES
            cut[q * tok:(q + 1) * tok, j * LANES:(j + 1) * LANES] = tokens_ref[:, column:column + LANES]
    out_ref[...] = lax.dot_general(
        chosen_ref[...], cut[...], (((0,), (0,)), ((), ())), preferred_element_type=jnp.float32
    ).astype(jnp.bfloat16)


def pack(chosen, tokens):
    tok, width = tokens.shape
    return pl.pallas_call(
        pack_kernel,
        out_shape=jax.ShapeDtypeStruct((chosen.shape[1], width // QUARTERS), jnp.bfloat16),
        in_specs=[VMEM, VMEM],
        out_specs=VMEM,
        scratch_shapes=[pltpu.VMEM((QUARTERS * tok, width // QUARTERS), jnp.bfloat16)],
        cost_estimate=pl.CostEstimate(flops=8_000_000_000, bytes_accessed=4 << 20, transcendentals=0),
        compiler_params=pltpu.CompilerParams(vmem_limit_bytes=8 << 20),
    )(chosen, tokens)


def weigh(ids_ref, gates_ref, chosen_ref, out_ref):
    top, tok = ids_ref.shape
    rows = out_ref.shape[1]
    wide = QUARTERS * tok
    ids = turned(ids_ref[...]).astype(jnp.int32)
    gates = turned(gates_ref[...])
    expert = lax.broadcasted_iota(jnp.int32, (tok, rows), 1) // PART
    weight = jnp.zeros((tok, rows), jnp.float32)
    for k in range(top):
        weight = jnp.where(expert == ids[:, k:k + 1], gates[:, k:k + 1], weight)
    high = weight.astype(jnp.bfloat16)
    low = (weight - high.astype(jnp.float32)).astype(jnp.bfloat16)
    for q in range(QUARTERS):
        part = slice(q * tok, (q + 1) * tok)
        chosen = chosen_ref[part, :]
        out_ref[part, :] = high * chosen
        out_ref[wide + q * tok:wide + (q + 1) * tok, :] = low * chosen


def combine_kernel(weights_ref, returned_ref, out_ref):
    tok = out_ref.shape[0]
    wide = QUARTERS * tok
    tiles = returned_ref.shape[1] // LANES
    both = jnp.dot(weights_ref[...], returned_ref[...], preferred_element_type=jnp.float32)
    total = (both[0:wide] + both[wide:2 * wide]).astype(jnp.bfloat16)
    for q in range(QUARTERS):
        for j in range(tiles):
            column = (j * QUARTERS + q) * LANES
            out_ref[:, column:column + LANES] = total[q * tok:(q + 1) * tok, j * LANES:(j + 1) * LANES]


def combine(weights, returned, tok):
    width = returned.shape[1] * QUARTERS
    return pl.pallas_call(
        combine_kernel,
        out_shape=jax.ShapeDtypeStruct((tok, width), jnp.bfloat16),
        in_specs=[VMEM, VMEM],
        out_specs=VMEM,
        compiler_params=pltpu.CompilerParams(vmem_limit_bytes=16 << 20),
    )(weights, returned)


def expert_kernel(
    ids_ref, gates_ref, chosen_ref, got_ref, gate_ref, up_ref, down_ref, out_ref, weights_ref, wide_buf
):
    rows = got_ref.shape[0]
    sources = rows // PART
    tiles = got_ref.shape[1] // LANES
    d_tile = QUARTERS * LANES

    weigh(ids_ref, gates_ref, chosen_ref, weights_ref)

    def unpack(j):
        wide_buf[j] = got_ref[:, j * LANES:(j + 1) * LANES].astype(jnp.float32)
        return jnp.concatenate(
            [
                jnp.concatenate(
                    [
                        wide_buf[j, pl.ds(q * CAPACITY + slot, sources, stride=PART), :].astype(jnp.bfloat16)
                        for q in range(QUARTERS)
                    ],
                    axis=1,
                )
                for slot in range(CAPACITY)
            ],
            axis=0,
        )

    gate_part = up_part = 0.0
    for j in range(tiles):
        piece = unpack(j)
        part = slice(j * d_tile, (j + 1) * d_tile)
        gate_part += jnp.dot(piece, gate_ref[part, :], preferred_element_type=jnp.float32)
        up_part += jnp.dot(piece, up_ref[part, :], preferred_element_type=jnp.float32)
    hidden = gate_part / (1.0 + jnp.exp(-gate_part)) * up_part
    hidden = hidden.astype(jnp.bfloat16)

    def scatter(n, produced):
        for slot in range(CAPACITY):
            for q in range(QUARTERS):
                wide_buf[n, pl.ds(q * CAPACITY + slot, sources, stride=PART), :] = produced[
                    slot * sources:(slot + 1) * sources, q * LANES:(q + 1) * LANES
                ]
        out_ref[:, n * LANES:(n + 1) * LANES] = wide_buf[n].astype(jnp.bfloat16)

    before = None
    for n in range(tiles):
        produced = jnp.dot(hidden, down_ref[:, n * d_tile:(n + 1) * d_tile], preferred_element_type=jnp.float32)
        if before is not None:
            scatter(n - 1, before)
        before = produced
    scatter(tiles - 1, before)


def expert_ffn(ids, gates, chosen, got, gate_matrix, up_matrix, down_matrix):
    rows, packed = got.shape
    top, tok = ids.shape
    return pl.pallas_call(
        expert_kernel,
        out_shape=(
            jax.ShapeDtypeStruct(got.shape, jnp.bfloat16),
            jax.ShapeDtypeStruct((2 * QUARTERS * tok, rows), jnp.bfloat16),
        ),
        in_specs=[VMEM] * 7,
        out_specs=(VMEM, VMEM),
        scratch_shapes=[
            pltpu.VMEM((packed // LANES, rows, LANES), jnp.float32),
        ],
        compiler_params=pltpu.CompilerParams(vmem_limit_bytes=14 << 20),
    )(ids, gates, chosen, got, gate_matrix, up_matrix, down_matrix)


def swap(messages, experts):
    parts = messages.reshape(experts, PART, messages.shape[1])
    moved = lax.all_to_all(parts, ("group", "local"), split_axis=0, concat_axis=0, tiled=True)
    return moved.reshape(messages.shape)


def on_device(tokens, expert_ids, gates, w_gate, w_up, w_down):
    experts = lax.axis_size("group") * lax.axis_size("local")
    ids = expert_ids.T.astype(jnp.float32)
    chosen = choose(ids, experts)
    got = swap(pack(chosen, tokens), experts)
    produced, weights = expert_ffn(ids, gates.T, chosen, got, w_gate[0], w_up[0], w_down[0])
    returned = swap(produced, experts)
    return combine(weights, returned, tokens.shape[0])


def solution(mesh):
    placed = (
        P(("group", "local"), None),
        P(("group", "local"), None),
        P(("group", "local"), None),
        P(("group", "local"), None, None),
        P(("group", "local"), None, None),
        P(("group", "local"), None, None),
    )
    return jax.shard_map(
        on_device,
        mesh=mesh,
        in_specs=placed,
        out_specs=P(("group", "local"), None),
        check_vma=False,
    )
```

```python
import jax
import jax.numpy as jnp
from jax import lax
from jax.experimental import pallas as pl
from jax.experimental.pallas import tpu as pltpu
from jax.sharding import PartitionSpec as P

CAPACITY = 2
QUARTERS = 4
PART = CAPACITY * QUARTERS
LANES = 128
ORDER = [x * 32 + y * 8 + z * 2 + c for c in range(2) for z in range(4) for y in range(4) for x in range(4)]
VMEM = pl.BlockSpec(memory_space=pltpu.VMEM)


def turned(values):
    tok = values.shape[1]
    a = lax.broadcasted_iota(jnp.int32, (tok, tok), 0)
    b = lax.broadcasted_iota(jnp.int32, (tok, tok), 1)
    return lax.dot_general(
        (a == b).astype(jnp.float32), values, (((1,), (1,)), ((), ())),
        precision=lax.Precision.HIGHEST, preferred_element_type=jnp.float32,
    )


def choose_kernel(ids_ref, out_ref):
    top, tok = ids_ref.shape
    rows = out_ref.shape[1]
    ids = turned(ids_ref[...]).astype(jnp.int32)
    row = lax.broadcasted_iota(jnp.int32, (tok, rows), 1)
    expert = row // PART
    picked = expert == ids[:, 0:1]
    for k in range(1, top):
        picked = picked | (expert == ids[:, k:k + 1])
    a = lax.broadcasted_iota(jnp.int32, (tok, tok), 0)
    b = lax.broadcasted_iota(jnp.int32, (tok, tok), 1)
    before = (b < a).astype(jnp.bfloat16)
    rank = jnp.dot(before, picked.astype(jnp.bfloat16), preferred_element_type=jnp.float32)
    slot = lax.rem(row, CAPACITY)
    quarter = lax.rem(row // CAPACITY, QUARTERS)
    chosen = picked & (rank == slot.astype(jnp.float32))
    for q in range(QUARTERS):
        out_ref[q * tok:(q + 1) * tok, :] = (chosen & (quarter == q)).astype(jnp.bfloat16)


def choose(ids, experts):
    tok = ids.shape[1]
    return pl.pallas_call(
        choose_kernel,
        out_shape=jax.ShapeDtypeStruct((QUARTERS * tok, experts * PART), jnp.bfloat16),
        in_specs=[VMEM],
        out_specs=VMEM,
        cost_estimate=pl.CostEstimate(flops=8_000_000_000, bytes_accessed=1 << 18, transcendentals=0),
        compiler_params=pltpu.CompilerParams(vmem_limit_bytes=8 << 20),
    )(ids)


def pack_kernel(chosen_ref, tokens_ref, out_ref, cut):
    tok = tokens_ref.shape[0]
    tiles = out_ref.shape[1] // LANES
    for q in range(QUARTERS):
        for j in range(tiles):
            column = (j * QUARTERS + q) * LANES
            cut[q * tok:(q + 1) * tok, j * LANES:(j + 1) * LANES] = tokens_ref[:, column:column + LANES]
    out_ref[...] = lax.dot_general(
        chosen_ref[...], cut[...], (((0,), (0,)), ((), ())), preferred_element_type=jnp.float32
    ).astype(jnp.bfloat16)


def pack(chosen, tokens):
    tok, width = tokens.shape
    return pl.pallas_call(
        pack_kernel,
        out_shape=jax.ShapeDtypeStruct((chosen.shape[1], width // QUARTERS), jnp.bfloat16),
        in_specs=[VMEM, VMEM],
        out_specs=VMEM,
        scratch_shapes=[pltpu.VMEM((QUARTERS * tok, width // QUARTERS), jnp.bfloat16)],
        cost_estimate=pl.CostEstimate(flops=8_000_000_000, bytes_accessed=4 << 20, transcendentals=0),
        compiler_params=pltpu.CompilerParams(vmem_limit_bytes=8 << 20),
    )(chosen, tokens)


def weigh(ids_ref, gates_ref, chosen_ref, out_ref):
    top, tok = ids_ref.shape
    rows = out_ref.shape[1]
    wide = QUARTERS * tok
    ids = turned(ids_ref[...]).astype(jnp.int32)
    gates = turned(gates_ref[...])
    expert = lax.broadcasted_iota(jnp.int32, (tok, rows), 1) // PART
    weight = jnp.zeros((tok, rows), jnp.float32)
    for k in range(top):
        weight = jnp.where(expert == ids[:, k:k + 1], gates[:, k:k + 1], weight)
    high = weight.astype(jnp.bfloat16)
    low = (weight - high.astype(jnp.float32)).astype(jnp.bfloat16)
    for q in range(QUARTERS):
        part = slice(q * tok, (q + 1) * tok)
        chosen = chosen_ref[part, :]
        out_ref[part, :] = high * chosen
        out_ref[wide + q * tok:wide + (q + 1) * tok, :] = low * chosen


def combine_kernel(weights_ref, returned_ref, out_ref):
    tok = out_ref.shape[0]
    wide = QUARTERS * tok
    tiles = returned_ref.shape[1] // LANES
    both = jnp.dot(weights_ref[...], returned_ref[...], preferred_element_type=jnp.float32)
    total = (both[0:wide] + both[wide:2 * wide]).astype(jnp.bfloat16)
    for q in range(QUARTERS):
        for j in range(tiles):
            column = (j * QUARTERS + q) * LANES
            out_ref[:, column:column + LANES] = total[q * tok:(q + 1) * tok, j * LANES:(j + 1) * LANES]


def combine(weights, returned, tok):
    width = returned.shape[1] * QUARTERS
    return pl.pallas_call(
        combine_kernel,
        out_shape=jax.ShapeDtypeStruct((tok, width), jnp.bfloat16),
        in_specs=[VMEM, VMEM],
        out_specs=VMEM,
        compiler_params=pltpu.CompilerParams(vmem_limit_bytes=16 << 20),
    )(weights, returned)


def expert_kernel(
    ids_ref, gates_ref, chosen_ref, got_ref, gate_ref, up_ref, down_ref, out_ref, weights_ref, wide_buf
):
    rows = got_ref.shape[0]
    sources = rows // PART
    tiles = got_ref.shape[1] // LANES
    d_tile = QUARTERS * LANES

    weigh(ids_ref, gates_ref, chosen_ref, weights_ref)

    def unpack(j):
        wide_buf[j] = got_ref[:, j * LANES:(j + 1) * LANES].astype(jnp.float32)
        return jnp.concatenate(
            [
                jnp.concatenate(
                    [
                        wide_buf[j, pl.ds(q * CAPACITY + slot, sources, stride=PART), :].astype(jnp.bfloat16)
                        for q in range(QUARTERS)
                    ],
                    axis=1,
                )
                for slot in range(CAPACITY)
            ],
            axis=0,
        )

    gate_part = up_part = 0.0
    for j in range(tiles):
        piece = unpack(j)
        part = slice(j * d_tile, (j + 1) * d_tile)
        gate_part += jnp.dot(piece, gate_ref[part, :], preferred_element_type=jnp.float32)
        up_part += jnp.dot(piece, up_ref[part, :], preferred_element_type=jnp.float32)
    hidden = gate_part / (1.0 + jnp.exp(-gate_part)) * up_part
    hidden = hidden.astype(jnp.bfloat16)

    def scatter(n, produced):
        for slot in range(CAPACITY):
            for q in range(QUARTERS):
                wide_buf[n, pl.ds(q * CAPACITY + slot, sources, stride=PART), :] = produced[
                    slot * sources:(slot + 1) * sources, q * LANES:(q + 1) * LANES
                ]
        out_ref[:, n * LANES:(n + 1) * LANES] = wide_buf[n].astype(jnp.bfloat16)

    before = None
    for n in range(tiles):
        produced = jnp.dot(hidden, down_ref[:, n * d_tile:(n + 1) * d_tile], preferred_element_type=jnp.float32)
        if before is not None:
            scatter(n - 1, before)
        before = produced
    scatter(tiles - 1, before)


def expert_ffn(ids, gates, chosen, got, gate_matrix, up_matrix, down_matrix):
    rows, packed = got.shape
    top, tok = ids.shape
    return pl.pallas_call(
        expert_kernel,
        out_shape=(
            jax.ShapeDtypeStruct(got.shape, jnp.bfloat16),
            jax.ShapeDtypeStruct((2 * QUARTERS * tok, rows), jnp.bfloat16),
        ),
        in_specs=[VMEM] * 7,
        out_specs=(VMEM, VMEM),
        scratch_shapes=[
            pltpu.VMEM((packed // LANES, rows, LANES), jnp.float32),
        ],
        compiler_params=pltpu.CompilerParams(vmem_limit_bytes=14 << 20),
    )(ids, gates, chosen, got, gate_matrix, up_matrix, down_matrix)


def swap(messages, experts):
    parts = messages.reshape(experts, PART, messages.shape[1])
    moved = lax.all_to_all(parts, ("group", "local"), axis_index_groups=[ORDER], split_axis=0, concat_axis=0, tiled=True)
    return moved.reshape(messages.shape)


def on_device(tokens, expert_ids, gates, w_gate, w_up, w_down):
    experts = lax.axis_size("group") * lax.axis_size("local")
    e = expert_ids
    message = (e & 1) * 64 + ((e >> 1) & 3) * 16 + ((e >> 3) & 3) * 4 + (e >> 5)
    ids = message.T.astype(jnp.float32)
    chosen = choose(ids, experts)
    got = swap(pack(chosen, tokens), experts)
    produced, weights = expert_ffn(ids, gates.T, chosen, got, w_gate[0], w_up[0], w_down[0])
    returned = swap(produced, experts)
    return combine(weights, returned, tokens.shape[0])


def solution(mesh):
    placed = (
        P(("group", "local"), None),
        P(("group", "local"), None),
        P(("group", "local"), None),
        P(("group", "local"), None, None),
        P(("group", "local"), None, None),
        P(("group", "local"), None, None),
    )
    return jax.shard_map(
        on_device,
        mesh=mesh,
        in_specs=placed,
        out_specs=P(("group", "local"), None),
        check_vma=False,
    )
```

```python
import jax
import jax.numpy as jnp
from jax import lax
from jax.experimental import pallas as pl
from jax.experimental.pallas import tpu as pltpu
from jax.sharding import PartitionSpec as P

CAPACITY = 2
QUARTERS = 4
PART = CAPACITY * QUARTERS
LANES = 128
ORDER = [
    x * 32 + (x + y) % 4 * 8 + (x + z) % 4 * 2 + c
    for c in range(2) for z in range(4) for y in range(4) for x in range(4)
]
VMEM = pl.BlockSpec(memory_space=pltpu.VMEM)


def turned(values):
    tok = values.shape[1]
    a = lax.broadcasted_iota(jnp.int32, (tok, tok), 0)
    b = lax.broadcasted_iota(jnp.int32, (tok, tok), 1)
    return lax.dot_general(
        (a == b).astype(jnp.float32), values, (((1,), (1,)), ((), ())),
        precision=lax.Precision.HIGHEST, preferred_element_type=jnp.float32,
    )


def choose_kernel(ids_ref, out_ref):
    top, tok = ids_ref.shape
    rows = out_ref.shape[1]
    ids = turned(ids_ref[...]).astype(jnp.int32)
    row = lax.broadcasted_iota(jnp.int32, (tok, rows), 1)
    expert = row // PART
    picked = expert == ids[:, 0:1]
    for k in range(1, top):
        picked = picked | (expert == ids[:, k:k + 1])
    a = lax.broadcasted_iota(jnp.int32, (tok, tok), 0)
    b = lax.broadcasted_iota(jnp.int32, (tok, tok), 1)
    before = (b < a).astype(jnp.bfloat16)
    rank = jnp.dot(before, picked.astype(jnp.bfloat16), preferred_element_type=jnp.float32)
    slot = lax.rem(row, CAPACITY)
    quarter = lax.rem(row // CAPACITY, QUARTERS)
    chosen = picked & (rank == slot.astype(jnp.float32))
    for q in range(QUARTERS):
        out_ref[q * tok:(q + 1) * tok, :] = (chosen & (quarter == q)).astype(jnp.bfloat16)


def choose(ids, experts):
    tok = ids.shape[1]
    return pl.pallas_call(
        choose_kernel,
        out_shape=jax.ShapeDtypeStruct((QUARTERS * tok, experts * PART), jnp.bfloat16),
        in_specs=[VMEM],
        out_specs=VMEM,
        cost_estimate=pl.CostEstimate(flops=8_000_000_000, bytes_accessed=1 << 18, transcendentals=0),
        compiler_params=pltpu.CompilerParams(vmem_limit_bytes=8 << 20),
    )(ids)


def pack_kernel(chosen_ref, tokens_ref, out_ref, cut):
    tok = tokens_ref.shape[0]
    tiles = out_ref.shape[1] // LANES
    for q in range(QUARTERS):
        for j in range(tiles):
            column = (j * QUARTERS + q) * LANES
            cut[q * tok:(q + 1) * tok, j * LANES:(j + 1) * LANES] = tokens_ref[:, column:column + LANES]
    out_ref[...] = lax.dot_general(
        chosen_ref[...], cut[...], (((0,), (0,)), ((), ())), preferred_element_type=jnp.float32
    ).astype(jnp.bfloat16)


def pack(chosen, tokens):
    tok, width = tokens.shape
    return pl.pallas_call(
        pack_kernel,
        out_shape=jax.ShapeDtypeStruct((chosen.shape[1], width // QUARTERS), jnp.bfloat16),
        in_specs=[VMEM, VMEM],
        out_specs=VMEM,
        scratch_shapes=[pltpu.VMEM((QUARTERS * tok, width // QUARTERS), jnp.bfloat16)],
        cost_estimate=pl.CostEstimate(flops=8_000_000_000, bytes_accessed=4 << 20, transcendentals=0),
        compiler_params=pltpu.CompilerParams(vmem_limit_bytes=8 << 20),
    )(chosen, tokens)


def weigh(ids_ref, gates_ref, chosen_ref, out_ref):
    top, tok = ids_ref.shape
    rows = out_ref.shape[1]
    wide = QUARTERS * tok
    ids = turned(ids_ref[...]).astype(jnp.int32)
    gates = turned(gates_ref[...])
    expert = lax.broadcasted_iota(jnp.int32, (tok, rows), 1) // PART
    weight = jnp.zeros((tok, rows), jnp.float32)
    for k in range(top):
        weight = jnp.where(expert == ids[:, k:k + 1], gates[:, k:k + 1], weight)
    high = weight.astype(jnp.bfloat16)
    low = (weight - high.astype(jnp.float32)).astype(jnp.bfloat16)
    for q in range(QUARTERS):
        part = slice(q * tok, (q + 1) * tok)
        chosen = chosen_ref[part, :]
        out_ref[part, :] = high * chosen
        out_ref[wide + q * tok:wide + (q + 1) * tok, :] = low * chosen


def combine_kernel(weights_ref, returned_ref, out_ref):
    tok = out_ref.shape[0]
    wide = QUARTERS * tok
    tiles = returned_ref.shape[1] // LANES
    both = jnp.dot(weights_ref[...], returned_ref[...], preferred_element_type=jnp.float32)
    total = (both[0:wide] + both[wide:2 * wide]).astype(jnp.bfloat16)
    for q in range(QUARTERS):
        for j in range(tiles):
            column = (j * QUARTERS + q) * LANES
            out_ref[:, column:column + LANES] = total[q * tok:(q + 1) * tok, j * LANES:(j + 1) * LANES]


def combine(weights, returned, tok):
    width = returned.shape[1] * QUARTERS
    return pl.pallas_call(
        combine_kernel,
        out_shape=jax.ShapeDtypeStruct((tok, width), jnp.bfloat16),
        in_specs=[VMEM, VMEM],
        out_specs=VMEM,
        compiler_params=pltpu.CompilerParams(vmem_limit_bytes=16 << 20),
    )(weights, returned)


def expert_kernel(
    ids_ref, gates_ref, chosen_ref, got_ref, gate_ref, up_ref, down_ref, out_ref, weights_ref, wide_buf
):
    rows = got_ref.shape[0]
    sources = rows // PART
    tiles = got_ref.shape[1] // LANES
    d_tile = QUARTERS * LANES

    weigh(ids_ref, gates_ref, chosen_ref, weights_ref)

    def unpack(j):
        wide_buf[j] = got_ref[:, j * LANES:(j + 1) * LANES].astype(jnp.float32)
        return jnp.concatenate(
            [
                jnp.concatenate(
                    [
                        wide_buf[j, pl.ds(q * CAPACITY + slot, sources, stride=PART), :].astype(jnp.bfloat16)
                        for q in range(QUARTERS)
                    ],
                    axis=1,
                )
                for slot in range(CAPACITY)
            ],
            axis=0,
        )

    gate_part = up_part = 0.0
    for j in range(tiles):
        piece = unpack(j)
        part = slice(j * d_tile, (j + 1) * d_tile)
        gate_part += jnp.dot(piece, gate_ref[part, :], preferred_element_type=jnp.float32)
        up_part += jnp.dot(piece, up_ref[part, :], preferred_element_type=jnp.float32)
    hidden = gate_part / (1.0 + jnp.exp(-gate_part)) * up_part
    hidden = hidden.astype(jnp.bfloat16)

    def scatter(n, produced):
        for slot in range(CAPACITY):
            for q in range(QUARTERS):
                wide_buf[n, pl.ds(q * CAPACITY + slot, sources, stride=PART), :] = produced[
                    slot * sources:(slot + 1) * sources, q * LANES:(q + 1) * LANES
                ]
        out_ref[:, n * LANES:(n + 1) * LANES] = wide_buf[n].astype(jnp.bfloat16)

    before = None
    for n in range(tiles):
        produced = jnp.dot(hidden, down_ref[:, n * d_tile:(n + 1) * d_tile], preferred_element_type=jnp.float32)
        if before is not None:
            scatter(n - 1, before)
        before = produced
    scatter(tiles - 1, before)


def expert_ffn(ids, gates, chosen, got, gate_matrix, up_matrix, down_matrix):
    rows, packed = got.shape
    top, tok = ids.shape
    return pl.pallas_call(
        expert_kernel,
        out_shape=(
            jax.ShapeDtypeStruct(got.shape, jnp.bfloat16),
            jax.ShapeDtypeStruct((2 * QUARTERS * tok, rows), jnp.bfloat16),
        ),
        in_specs=[VMEM] * 7,
        out_specs=(VMEM, VMEM),
        scratch_shapes=[
            pltpu.VMEM((packed // LANES, rows, LANES), jnp.float32),
        ],
        compiler_params=pltpu.CompilerParams(vmem_limit_bytes=14 << 20),
    )(ids, gates, chosen, got, gate_matrix, up_matrix, down_matrix)


def swap(messages, experts):
    parts = messages.reshape(experts, PART, messages.shape[1])
    moved = lax.all_to_all(parts, ("group", "local"), axis_index_groups=[ORDER], split_axis=0, concat_axis=0, tiled=True)
    return moved.reshape(messages.shape)


def on_device(tokens, expert_ids, gates, w_gate, w_up, w_down):
    experts = lax.axis_size("group") * lax.axis_size("local")
    e = expert_ids
    x = e >> 5
    message = (e & 1) * 64 + (((e >> 1) - x) & 3) * 16 + (((e >> 3) - x) & 3) * 4 + x
    ids = message.T.astype(jnp.float32)
    chosen = choose(ids, experts)
    got = swap(pack(chosen, tokens), experts)
    produced, weights = expert_ffn(ids, gates.T, chosen, got, w_gate[0], w_up[0], w_down[0])
    returned = swap(produced, experts)
    return combine(weights, returned, tokens.shape[0])


def solution(mesh):
    placed = (
        P(("group", "local"), None),
        P(("group", "local"), None),
        P(("group", "local"), None),
        P(("group", "local"), None, None),
        P(("group", "local"), None, None),
        P(("group", "local"), None, None),
    )
    return jax.shard_map(
        on_device,
        mesh=mesh,
        in_specs=placed,
        out_specs=P(("group", "local"), None),
        check_vma=False,
    )
```
